256 devices in a mesh: row: 8 (over z_lo, x), col: 32 (over y, z_hi, core).
Axes of the slice: x: 4, y: 4, z: 8 (z_hi: 4, z_lo: 2; z = z_hi * 2 + z_lo), core: 2. Of those that a mesh axis runs over, the one named last changes fastest.
Arguments:
- tokens: bfloat16 [4096, 6144], P('row', 'col'), may hold values from -6 to 6
- w_qkvg: bfloat16 [6144, 64, 512], P('row', 'col'), may hold values from -0.078125 to 0.078125
- w_out: bfloat16 [64, 128, 6144], P('col', None, 'row'), may hold values from -0.125 to 0.125
- norm_gain: float32 [64, 128], P('col'), may hold values from 0.1 to 1.9
- decay_index: int32 [64], P('col'), may hold values from 0 to 15
Outputs:
- mixed: bfloat16 [4096, 6144], P('row', 'col')
The draws below stay inside these ranges and needn't reach their ends.
All inputs are finite; a program needn't handle non-finite values.
Results may differ from the reference program's by a relative error of at most 0.02.
Values may be sent and summed in bfloat16 or wider, within the bound.
No kernel may reach another device: no remote copies, remote signals or barrier semaphores. Data moves between devices by JAX's collectives and lax.ppermute only.
A program may use at most 128 MiB of HBM per device.

```python
import math
import jax
import jax.numpy as jnp
from jax import lax

D = 6144
H = 64
DH = 128
NSLOPE = 16
TOKENS = 4096


def with_ends(array, own_key, smallest, high):
    dims = array.shape
    spot = [jax.random.randint(jax.random.fold_in(own_key, axis), (), 0, dims[axis]) for axis in range(len(dims))]
    array = array.at[tuple(spot)].set(smallest)
    longest = dims.index(max(dims))
    spot[longest] = (spot[longest] + 1) % dims[longest]
    return array.at[tuple(spot)].set(high)


def raised(array, rng, source, target, blocks, factor):
    owner, partner = [(jnp.arange(array.shape[axis_at]) // (array.shape[axis_at] // blocks)).reshape([-1 if axis == axis_at else 1 for axis in range(array.ndim)]) for axis_at in (source, target)]
    chosen = jax.random.permutation(rng, blocks)[partner]
    strong = (owner == chosen) | (owner == (partner + blocks // 2) % blocks)
    return jnp.where(strong, factor * array, array)


def steps_of(key, dims, shards, low, largest):
    loudness, own = 1.0, jax.random.fold_in(key, 6)
    for position, blocks in shards:
        heights = jnp.exp(jax.random.uniform(jax.random.fold_in(own, position), (blocks,), jnp.float32, low / len(shards), largest / len(shards)))
        loudness = loudness * jnp.repeat(heights, dims[position] // blocks).reshape([-1 if axis == position else 1 for axis in range(len(dims))])
    return loudness


def scatter_about(stream_key, extent, deviation, most, shards=(), kind=jnp.bfloat16):
    result = deviation * jax.random.normal(stream_key, extent, jnp.float32)
    if shards:
        result = result * steps_of(stream_key, extent, shards, -0.22, 0.18)
    return jnp.clip(result, -most, most).astype(kind)


def bell_draw_with(own_key, dims, spread, reach, shards, heavy, kind=jnp.bfloat16):
    result = spread * jax.random.normal(own_key, dims, jnp.float32)
    if shards:
        result = result * steps_of(own_key, dims, shards, -0.22, 0.18)
    return jnp.clip(raised(result, jax.random.fold_in(own_key, 3), *heavy), -reach, reach).astype(kind)


def setup_inputs(seed: int = 0) -> dict:
    seeds = jax.random.split(jax.random.key(seed), 6)
    return {
        "tokens": scatter_about(seeds[0], (TOKENS, D), 1.0, 6.0, ((0, 8), (1, 32))),
        "w_qkvg": scatter_about(seeds[1], (D, H, 4 * DH), D ** -0.5, 0.078125, ((0, 8), (1, 32))),
        "w_out": bell_draw_with(seeds[2], (H, DH, D), (H * DH) ** -0.5, 0.125, ((0, 32), (2, 8)), (0, 2, 32, 2.75)),
        "norm_gain": jnp.clip(1.0 + 0.18 * jax.random.normal(seeds[3], (H, DH), jnp.float32), 0.1, 1.9),
        "decay_index": with_ends(jax.random.randint(seeds[4], (H,), 0, NSLOPE), jax.random.fold_in(seeds[4], 1), 0, NSLOPE - 1).astype(jnp.int32),
    }


def decay_rates(index_vec, total_rows):
    exponent = index_vec.astype(jnp.float32) / (NSLOPE - 1)
    fast_rate = 1.0 / 32.0
    slow_rate = 0.5 / total_rows
    return fast_rate * jnp.exp(exponent * math.log(slow_rate / fast_rate))

def reference(tokens, w_qkvg, w_out, norm_gain, decay_index):
    projected = jnp.dot(tokens, w_qkvg.reshape(D, H * 4 * DH), preferred_element_type=jnp.float32)
    projected = projected.astype(jnp.bfloat16).reshape(TOKENS, H, 4, DH)
    activated = jax.nn.silu(projected[:, :, :3].astype(jnp.float32))
    gate_part = projected[:, :, 3].astype(jnp.float32)
    rate_vec = decay_rates(decay_index, TOKENS)
    positions = jnp.arange(TOKENS, dtype=jnp.float32)
    distance = positions[:, None] - positions[None, :]

    def one_head(head_data):
        queries, keys_act, values_act, rate_one = head_data
        weight = jnp.where(distance >= 0, jnp.exp(-rate_one * jnp.maximum(distance, 0.0)), 0.0)
        scores = jnp.dot(queries, keys_act.T, precision=lax.Precision.HIGHEST) * weight
        return jnp.dot(scores, values_act, precision=lax.Precision.HIGHEST)
    attended = lax.map(one_head, (activated[:, :, 0].transpose(1, 0, 2), activated[:, :, 1].transpose(1, 0, 2), activated[:, :, 2].transpose(1, 0, 2), rate_vec))
    mean_square = lax.optimization_barrier(jnp.mean(attended * attended, axis=-1, keepdims=True))
    normed = attended * lax.rsqrt(mean_square + 1e-06) * norm_gain[:, None, :]
    hidden = (normed * jax.nn.sigmoid(gate_part.transpose(1, 0, 2))).astype(jnp.bfloat16)
    flat_hidden = hidden.transpose(1, 0, 2).reshape(TOKENS, H * DH)
    mixed = jnp.dot(flat_hidden, w_out.reshape(H * DH, D), preferred_element_type=jnp.float32)
    return mixed.astype(jnp.bfloat16)
```

```python
import math

import jax
import jax.numpy as jnp
import numpy as np
from jax import lax
from jax.sharding import Mesh
from jax.sharding import PartitionSpec as P

NSLOPE = 16
AXES = ("zl", "x", "y", "zh", "core")
SIZES = (2, 4, 4, 4, 2)
BF = jnp.bfloat16
F32 = jnp.float32


def moves(target):
    pairs = []
    for flat in range(int(np.prod(SIZES))):
        place = [int(v) for v in np.unravel_index(flat, SIZES)]
        there = target(*place)
        if there is not None:
            pairs.append((flat, int(np.ravel_multi_index(there, SIZES))))
    return pairs


def send(array, target):
    return lax.ppermute(array, AXES, moves(target))


def along_x(step):
    return lambda zl, x, y, zh, c: (zl, (x + step) % 4, y, zh, c)


def along_y(step):
    return lambda zl, x, y, zh, c: (zl, x, (y + step) % 4, zh, c)


def along_zh(step):
    return lambda zl, x, y, zh, c: (zl, x, y, (zh + step) % 4, c)


def other_zl(zl, x, y, zh, c):
    return (1 - zl, x, y, zh, c)


def other_core(zl, x, y, zh, c):
    return (zl, x, y, zh, 1 - c)


def later_row(step):
    def target(zl, x, y, zh, c):
        row = zl * 4 + x + step
        return (row // 4, row % 4, y, zh, c) if row < 8 else None

    return target


def tokens_to_half(zl, x, y, zh, c):
    half = y // 2
    return (half, x, (zl ^ half) * 2 + y % 2, zh, c)


def w_out_to_columns(zl, x, y, zh, c):
    row = zl * 4 + x
    return (row % 2, y, row // 2, zh, c)


def gather_x(block):
    place = lax.axis_index("x")
    rows, columns = block.shape
    half = rows // 2
    low, high = block[:half], block[half:]
    left_low = send(low, along_x(1))
    right_high = send(high, along_x(-1))
    left_high = send(high, along_x(1))
    right_low = send(low, along_x(-1))
    far_low = send(left_low, along_x(1))
    far_high = send(right_high, along_x(-1))
    whole = jnp.zeros((4 * rows, columns), block.dtype)
    left = (place + 3) % 4 * rows
    right = (place + 1) % 4 * rows
    far = (place + 2) % 4 * rows
    for piece, start in (
        (block, place * rows),
        (left_low, left),
        (left_high, left + half),
        (right_low, right),
        (right_high, right + half),
        (far_low, far),
        (far_high, far + half),
    ):
        whole = lax.dynamic_update_slice(whole, piece, (start, 0))
    return whole


def decay_rates(index_vec, total_rows):
    exponent = index_vec.astype(F32) / (NSLOPE - 1)
    fast_rate = 1.0 / 32.0
    slow_rate = 0.5 / total_rows
    return fast_rate * jnp.exp(exponent * math.log(slow_rate / fast_rate))


def local(tokens, w_qkvg, w_out, norm_gain, decay_index):
    rows = tokens.shape[0]
    heads = w_qkvg.shape[1]
    size = w_qkvg.shape[2] // 4
    core = lax.axis_index("core")
    zh = lax.axis_index("zh")
    y = lax.axis_index("y")

    moved = send(tokens, tokens_to_half)
    gathered = lax.all_gather(moved, ("y", "zh", "core"), axis=1, tiled=True)
    width = gathered.shape[1] // 2
    mine, theirs = gathered[:, :width], gathered[:, width:]

    parts = w_qkvg.reshape(-1, heads, 4, size)
    kv_block = parts[:, :, 1:3].reshape(-1, heads * 2 * size)
    qg_block = jnp.stack([parts[:, :, 0], parts[:, :, 3]], axis=2).reshape(-1, heads * 2 * size)
    weight_cols = gather_x(jnp.concatenate([kv_block, qg_block], axis=1))
    w_kv, w_qg = weight_cols[:, : heads * 2 * size], weight_cols[:, heads * 2 * size :]

    w_out_moved = send(w_out.reshape(heads * size, -1), w_out_to_columns)
    w_out_all = lax.all_gather(w_out_moved, ("zl", "x"), axis=0, tiled=True)

    def half_dot(a, b):
        return jnp.dot(a, b, preferred_element_type=F32)

    kv_sent = send(half_dot(theirs, w_kv).astype(BF), other_zl)
    qg_sent = send(half_dot(theirs, w_qg).astype(BF), other_zl)
    kv = (half_dot(mine, w_kv) + kv_sent.astype(F32)).astype(BF).astype(F32)
    qg = (half_dot(mine, w_qg) + qg_sent.astype(F32)).astype(BF).astype(F32)

    kv = jax.nn.silu(kv).reshape(rows, heads, 2, size)
    keys_act, values_act = kv[:, :, 0], kv[:, :, 1].astype(BF)
    rate_vec = decay_rates(decay_index, rows * 8)
    local_pos = jnp.arange(rows, dtype=F32)
    state_weight = jnp.exp(-rate_vec[None, :] * (rows - 1.0 - local_pos)[:, None])
    local_state = jnp.einsum(
        "shd,she->hde",
        (keys_act * state_weight[:, :, None]).astype(BF),
        values_act,
        preferred_element_type=F32,
    ).astype(BF)
    keys_act = keys_act.astype(BF)
    carried = jnp.zeros(local_state.shape, F32)
    for step in range(1, 8):
        earlier = send(local_state, later_row(step)).astype(F32)
        carried += jnp.exp(-rate_vec * (rows * (step - 1.0)))[:, None, None] * earlier

    qg = qg.reshape(rows, heads, 2, size)
    queries, gate_part = jax.nn.silu(qg[:, :, 0]).astype(BF), qg[:, :, 1]
    distance = local_pos[:, None] - local_pos[None, :]
    weight = jnp.where(
        distance[None] >= 0,
        jnp.exp(-rate_vec[:, None, None] * jnp.maximum(distance, 0.0)[None]),
        0.0,
    )
    scores = jnp.einsum("thd,shd->hts", queries, keys_act, preferred_element_type=F32) * weight
    inner_part = jnp.einsum(
        "hts,shd->thd", scores.astype(BF), values_act, preferred_element_type=F32
    )
    entry_decay = jnp.exp(-rate_vec[None, :] * (local_pos[:, None] + 1.0))
    carried_part = entry_decay[:, :, None] * jnp.einsum(
        "thd,hde->the", queries, carried.astype(BF), preferred_element_type=F32
    )
    attended = inner_part + carried_part
    mean_square = jnp.mean(attended * attended, axis=-1, keepdims=True)
    normed = attended * lax.rsqrt(mean_square + 1e-06) * norm_gain[None]
    hidden = (normed * jax.nn.sigmoid(gate_part)).astype(BF).reshape(rows, heads * size)

    hidden_all = jnp.zeros((rows, 4 * heads * size), BF)
    hidden_all = lax.dynamic_update_slice(hidden_all, hidden, (0, y * heads * size))
    for step in (2, 1, 3):
        piece = send(hidden, along_y(step))
        hidden_all = lax.dynamic_update_slice(hidden_all, piece, (0, (y + 4 - step) % 4 * heads * size))

    depth = 4 * heads * size
    wide = [
        half_dot(hidden_all, w_out_all[part * depth : (part + 1) * depth]).reshape(rows, 2, 2, -1)
        for part in range(2)
    ]
    blocks = jnp.stack([wide[part][:, turn] for part in range(2) for turn in range(2)])
    kept = jnp.where(core == 0, blocks[:, :, 0], blocks[:, :, 1])
    given = jnp.where(core == 0, blocks[:, :, 1], blocks[:, :, 0]).astype(BF)
    summed = kept + send(given, other_core).astype(F32)
    total = lax.dynamic_index_in_dim(summed, zh, 0, False)
    outgoing = summed.astype(BF)
    for step in (2, 1, 3):
        piece = lax.dynamic_index_in_dim(outgoing, (zh + step) % 4, 0, False)
        total += send(piece, along_zh(step)).astype(F32)
    return total.astype(BF)


def solution(mesh):
    fine = Mesh(mesh.devices.reshape(SIZES), AXES)
    row, col = ("zl", "x"), ("y", "zh", "core")
    in_specs = (P(row, col), P(row, col, None), P(col, None, row), P(col, None), P(col))
    return jax.shard_map(
        local, mesh=fine, in_specs=in_specs, out_specs=P(row, col), check_vma=False
    )
```

```python
import math

import jax
import jax.numpy as jnp
import numpy as np
from jax import lax
from jax.sharding import Mesh
from jax.sharding import PartitionSpec as P

NSLOPE = 16
AXES = ("zl", "x", "y", "zh", "core")
SIZES = (2, 4, 4, 4, 2)
BF = jnp.bfloat16
F32 = jnp.float32


def moves(target):
    pairs = []
    for flat in range(int(np.prod(SIZES))):
        place = [int(v) for v in np.unravel_index(flat, SIZES)]
        there = target(*place)
        if there is not None:
            pairs.append((flat, int(np.ravel_multi_index(there, SIZES))))
    return pairs


def send(array, target):
    return lax.ppermute(array, AXES, moves(target))


def along_x(step):
    return lambda zl, x, y, zh, c: (zl, (x + step) % 4, y, zh, c)


def along_y(step):
    return lambda zl, x, y, zh, c: (zl, x, (y + step) % 4, zh, c)


def along_zh(step):
    return lambda zl, x, y, zh, c: (zl, x, y, (zh + step) % 4, c)


def other_zl(zl, x, y, zh, c):
    return (1 - zl, x, y, zh, c)


def other_core(zl, x, y, zh, c):
    return (zl, x, y, zh, 1 - c)


def later_half(zl, x, y, zh, c):
    return (1, x, y, zh, c) if zl == 0 else None


def tokens_to_half(zl, x, y, zh, c):
    half = y // 2
    return (half, x, (zl ^ half) * 2 + y % 2, zh, c)


def w_out_to_columns(zl, x, y, zh, c):
    there = zl * 2 + x // 2
    apart = y ^ there
    return (apart // 2, (apart % 2) * 2 + x % 2, there, zh, c)


def gather_ring(block, axis, along, half):
    left = send(block, along(1))
    right = send(block, along(-1))
    far_low = send(left[:half], along(1))
    far_high = send(right[half:], along(-1))
    place = lax.axis_index(axis)
    return (
        (block, 0, place),
        (left, 0, (place + 3) % 4),
        (right, 0, (place + 1) % 4),
        (far_low, 0, (place + 2) % 4),
        (far_high, half, (place + 2) % 4),
    )


def after(array, other):
    return array + other[(0,) * other.ndim] * jnp.zeros((), array.dtype)


def decay_rates(index_vec, total_rows):
    exponent = index_vec.astype(F32) / (NSLOPE - 1)
    fast_rate = 1.0 / 32.0
    slow_rate = 0.5 / total_rows
    return fast_rate * jnp.exp(exponent * math.log(slow_rate / fast_rate))


def local(tokens, w_qkvg, w_out, norm_gain, decay_index):
    rows = tokens.shape[0]
    heads = w_qkvg.shape[1]
    size = w_qkvg.shape[2] // 4
    core = lax.axis_index("core")
    zh = lax.axis_index("zh")
    y = lax.axis_index("y")

    w_block = w_qkvg.reshape(w_qkvg.shape[0], -1)
    weight_cols = lax.all_gather(w_block, "x", axis=0, tiled=True)

    moved = send(tokens.T, tokens_to_half)
    depth, across = moved.shape
    stacked = jnp.zeros((4, depth, across), BF)
    stacked = lax.dynamic_update_slice(stacked, moved[None], (zh, 0, 0))
    for step in (2, 1, 3):
        piece = send(moved, along_zh(step))
        stacked = lax.dynamic_update_slice(stacked, piece[None], ((zh + 4 - step) % 4, 0, 0))
    gathered = jnp.zeros((4, 4, 2, depth, across), BF)
    for piece, start, place in gather_ring(stacked, "y", along_y, 2):
        for part, owner in ((piece, core), (send(piece, other_core), 1 - core)):
            gathered = lax.dynamic_update_slice(
                gathered, part[None, :, None], (place, start, owner, 0, 0)
            )
    gathered = gathered.reshape(2, 16 * depth, across)
    mine, theirs = gathered[0], gathered[1]

    w_out_block = after(w_out.reshape(heads * size, -1), piece)
    w_out_moved = send(w_out_block, w_out_to_columns)
    w_out_pair = jnp.stack([w_out_moved, send(w_out_moved, other_zl)])
    w_out_all = lax.all_gather(w_out_pair, "x", axis=0, tiled=True)

    def half_dot(a, b):
        return jnp.dot(a, b, preferred_element_type=F32)

    def projection(a):
        return lax.dot_general(
            a, weight_cols, (((0,), (0,)), ((), ())), preferred_element_type=F32
        )

    def columns(array, parts):
        return jnp.concatenate(
            [array[:, (4 * h + p) * size : (4 * h + p + 1) * size] for h in range(heads) for p in parts],
            axis=1,
        )

    own_part, other_part = projection(mine), projection(theirs).astype(BF)
    kv_sent = send(columns(other_part, (1, 2)), other_zl)
    qg_sent = send(columns(other_part, (0, 3)), other_zl)
    kv = (columns(own_part, (1, 2)) + kv_sent.astype(F32)).astype(BF).astype(F32)
    qg = (columns(own_part, (0, 3)) + qg_sent.astype(F32)).astype(BF).astype(F32)

    kv = jax.nn.silu(kv).reshape(rows, heads, 2, size)
    keys_act, values_act = kv[:, :, 0], kv[:, :, 1].astype(BF)
    rate_vec = decay_rates(decay_index, rows * 8)
    local_pos = jnp.arange(rows, dtype=F32)
    state_weight = jnp.exp(-rate_vec[None, :] * (rows - 1.0 - local_pos)[:, None])
    local_state = jnp.einsum(
        "shd,she->hde",
        (keys_act * state_weight[:, :, None]).astype(BF),
        values_act,
        preferred_element_type=F32,
    ).astype(BF)
    keys_act = keys_act.astype(BF)
    place = lax.axis_index("x")

    def power(count):
        return jnp.exp(-rate_vec * (rows * 1.0) * count)[:, None, None]

    carried = jnp.zeros(local_state.shape, F32)
    total = power((3 - place).astype(F32)) * local_state.astype(F32)
    for step in (2, 1, 3):
        earlier = send(local_state, along_x(step)).astype(F32)
        carried += jnp.where(place >= step, power(step - 1.0), 0.0) * earlier
        total += power((3 - (place + 4 - step) % 4).astype(F32)) * earlier
    carried += power(place.astype(F32)) * send(total.astype(BF), later_half).astype(F32)

    qg = qg.reshape(rows, heads, 2, size)
    queries, gate_part = jax.nn.silu(qg[:, :, 0]).astype(BF), qg[:, :, 1]
    distance = local_pos[:, None] - local_pos[None, :]
    weight = jnp.where(
        distance[None] >= 0,
        jnp.exp(-rate_vec[:, None, None] * jnp.maximum(distance, 0.0)[None]),
        0.0,
    )
    scores = jnp.einsum("thd,shd->hts", queries, keys_act, preferred_element_type=F32) * weight
    inner_part = jnp.einsum(
        "hts,shd->thd", scores.astype(BF), values_act, preferred_element_type=F32
    )
    entry_decay = jnp.exp(-rate_vec[None, :] * (local_pos[:, None] + 1.0))
    carried_part = entry_decay[:, :, None] * jnp.einsum(
        "thd,hde->the", queries, carried.astype(BF), preferred_element_type=F32
    )
    attended = inner_part + carried_part
    mean_square = jnp.mean(attended * attended, axis=-1, keepdims=True)
    normed = attended * lax.rsqrt(mean_square + 1e-06) * norm_gain[None]
    hidden = (normed * jax.nn.sigmoid(gate_part)).astype(BF).reshape(rows, heads * size)

    def slot(origin):
        apart = origin ^ y
        return (apart % 2 * 2 + (apart // 2 ^ lax.axis_index("zl"))) * heads * size

    hidden_all = jnp.zeros((rows, 4 * heads * size), BF)
    hidden_all = lax.dynamic_update_slice(hidden_all, hidden, (0, slot(y)))
    for step in (2, 1, 3):
        piece = send(hidden, along_y(step))
        hidden_all = lax.dynamic_update_slice(hidden_all, piece, (0, slot((y + 4 - step) % 4)))

    span = 2 * heads * size
    w_out_all = w_out_all.reshape(4, span, -1)
    near, far = hidden_all[:, :span], hidden_all[:, span:]
    wide = [half_dot(near, w_out_all[part]) + half_dot(far, w_out_all[2 + part]) for part in range(2)]
    wide = [array.reshape(rows, 2, 2, -1) for array in wide]
    blocks = jnp.stack([wide[part][:, turn] for part in range(2) for turn in range(2)])
    kept = jnp.where(core == 0, blocks[:, :, 0], blocks[:, :, 1])
    given = jnp.where(core == 0, blocks[:, :, 1], blocks[:, :, 0]).astype(BF)
    summed = kept + send(given, other_core).astype(F32)
    total = lax.dynamic_index_in_dim(summed, zh, 0, False)
    outgoing = summed.astype(BF)
    for step in (2, 1, 3):
        piece = lax.dynamic_index_in_dim(outgoing, (zh + step) % 4, 0, False)
        total += send(piece, along_zh(step)).astype(F32)
    return total.astype(BF)


def solution(mesh):
    fine = Mesh(mesh.devices.reshape(SIZES), AXES)
    row, col = ("zl", "x"), ("y", "zh", "core")
    in_specs = (P(row, col), P(row, col, None), P(col, None, row), P(col, None), P(col))
    return jax.shard_map(
        local, mesh=fine, in_specs=in_specs, out_specs=P(row, col), check_vma=False
    )
```

```python
import math

import jax
import jax.numpy as jnp
import numpy as np
from jax import lax
from jax.sharding import Mesh
from jax.sharding import PartitionSpec as P

NSLOPE = 16
AXES = ("zl", "x", "y", "zh", "core")
SIZES = (2, 4, 4, 4, 2)
BF = jnp.bfloat16
F32 = jnp.float32


def moves(target):
    pairs = []
    for flat in range(int(np.prod(SIZES))):
        place = [int(v) for v in np.unravel_index(flat, SIZES)]
        there = target(*place)
        if there is not None:
            pairs.append((flat, int(np.ravel_multi_index(there, SIZES))))
    return pairs


def send(array, target):
    return lax.ppermute(array, AXES, moves(target))


def along_x(step):
    return lambda zl, x, y, zh, c: (zl, (x + step) % 4, y, zh, c)


def along_y(step):
    return lambda zl, x, y, zh, c: (zl, x, (y + step) % 4, zh, c)


def along_zh(step):
    return lambda zl, x, y, zh, c: (zl, x, y, (zh + step) % 4, c)


def other_zl(zl, x, y, zh, c):
    return (1 - zl, x, y, zh, c)


def other_core(zl, x, y, zh, c):
    return (zl, x, y, zh, 1 - c)


def later_half(zl, x, y, zh, c):
    return (1, x, y, zh, c) if zl == 0 else None


def tokens_to_half(zl, x, y, zh, c):
    half = y // 2
    return (half, x, (zl ^ half) * 2 + y % 2, zh, c)


def w_out_to_columns(high):
    def target(zl, x, y, zh, c):
        return (zl, (y % 2) * 2 + x % 2, zl * 2 + x // 2, zh, c) if y // 2 == high else None

    return target


def w_out_to_other_zl(zl, x, y, zh, c):
    return (1 - zl, x, y, zh, c) if y // 2 == zl else None


def gather_ring(block, axis, along, half, other):
    left = send(block, along(1))
    right = send(block, along(-1))
    far_low = send(after(left[:half], other), along(1))
    far_high = send(right[half:], along(-1))
    place = lax.axis_index(axis)
    return (
        (block, 0, place),
        (left, 0, (place + 3) % 4),
        (right, 0, (place + 1) % 4),
        (far_low, 0, (place + 2) % 4),
        (far_high, half, (place + 2) % 4),
    )


def after(array, other):
    return array + other[(0,) * other.ndim] * jnp.zeros((), array.dtype)


def decay_rates(index_vec, total_rows):
    exponent = index_vec.astype(F32) / (NSLOPE - 1)
    fast_rate = 1.0 / 32.0
    slow_rate = 0.5 / total_rows
    return fast_rate * jnp.exp(exponent * math.log(slow_rate / fast_rate))


def local(tokens, w_qkvg, w_out, norm_gain, decay_index):
    rows = tokens.shape[0]
    heads = w_qkvg.shape[1]
    size = w_qkvg.shape[2] // 4
    core = lax.axis_index("core")
    zh = lax.axis_index("zh")
    y = lax.axis_index("y")

    w_block = w_qkvg.reshape(2, 2, tokens.shape[1], -1)
    kv_cuts = [(4 * h + 1, 4 * h + 3) for h in range(heads)]
    qg_cuts = [(0, 1)] + [(4 * h + 3, 4 * h + 5) for h in range(heads - 1)] + [(4 * heads - 1, 4 * heads)]
    w_block = jnp.concatenate(
        [w_block[..., low * size : high * size] for low, high in kv_cuts + qg_cuts], axis=-1
    )
    w_block = jnp.stack(
        [jnp.where(core == own, w_block[:, 0], w_block[:, 1]) for own in range(2)], axis=1
    ).reshape(w_qkvg.shape[0], -1)
    weight_cols = lax.all_gather(w_block, "x", axis=0, tiled=True)

    w_out_block = w_out.reshape(heads * size, -1)
    w_out_moved = jnp.stack([send(w_out_block, w_out_to_columns(high)) for high in range(2)])

    moved = send(tokens.T, tokens_to_half)
    depth, across = moved.shape
    stacked = jnp.zeros((4, depth, across), BF)
    stacked = lax.dynamic_update_slice(stacked, moved[None], (zh, 0, 0))
    for step in (2, 1, 3):
        piece = send(moved, along_zh(step))
        stacked = lax.dynamic_update_slice(stacked, piece[None], ((zh + 4 - step) % 4, 0, 0))
    gathered = jnp.zeros((4, 4, 2, depth, across), BF)
    swapped = []
    for piece, start, place in gather_ring(stacked, "y", along_y, 2, w_out_moved):
        swapped.append(send(piece, other_core))
        both = jnp.stack([piece, swapped[-1]], axis=1)
        gathered = lax.dynamic_update_slice(gathered, both[None], (place, start, 0, 0, 0))
    gathered = gathered.reshape(2, 16 * depth, across)
    mine, theirs = gathered[0], gathered[1]

    w_out_pair = w_out_moved + send(w_out_moved, w_out_to_other_zl)
    w_out_all = lax.all_gather(w_out_pair, "x", axis=0, tiled=True)
    weight_cols = after(weight_cols, swapped[0])

    def projection(a, b):
        return lax.dot_general(a, b, (((0,), (0,)), ((), ())), preferred_element_type=F32)

    w_kv, w_qg = jnp.split(weight_cols, 2, axis=1)
    kv_theirs = projection(theirs, w_kv).astype(BF)
    kv_sent = send(kv_theirs, other_zl)
    qg_sent = send(projection(theirs, w_qg).astype(BF), other_zl)
    kv_own, qg_own = jnp.split(projection(mine, weight_cols), 2, axis=1)
    kv = (kv_own + kv_sent.astype(F32)).astype(BF).astype(F32)
    qg = (qg_own + qg_sent.astype(F32)).astype(BF).astype(F32)

    kv = jax.nn.silu(kv).reshape(rows, heads, 2, size)
    keys_act, values_act = kv[:, :, 0], kv[:, :, 1].astype(BF)
    rate_vec = decay_rates(decay_index, rows * 8)
    local_pos = jnp.arange(rows, dtype=F32)
    state_weight = jnp.exp(-rate_vec[None, :] * (rows - 1.0 - local_pos)[:, None])
    local_state = jnp.einsum(
        "shd,she->hde",
        (keys_act * state_weight[:, :, None]).astype(BF),
        values_act,
        preferred_element_type=F32,
    ).astype(BF)
    keys_act = keys_act.astype(BF)
    place = lax.axis_index("x")

    def power(count):
        return jnp.exp(-rate_vec * (rows * 1.0) * count)[:, None, None]

    carried = jnp.zeros(local_state.shape, F32)
    total = power((3 - place).astype(F32)) * local_state.astype(F32)
    for step in (2, 1, 3):
        earlier = send(local_state, along_x(step)).astype(F32)
        carried += jnp.where(place >= step, power(step - 1.0), 0.0) * earlier
        total += power((3 - (place + 4 - step) % 4).astype(F32)) * earlier
    carried += power(place.astype(F32)) * send(total.astype(BF), later_half).astype(F32)

    qg = after(qg, local_state).reshape(rows, heads, 2, size)
    queries, gate_part = jax.nn.silu(qg[:, :, 0]).astype(BF), qg[:, :, 1]
    distance = local_pos[:, None] - local_pos[None, :]
    weight = jnp.where(
        distance[None] >= 0,
        jnp.exp(-rate_vec[:, None, None] * jnp.maximum(distance, 0.0)[None]),
        0.0,
    )
    scores = jnp.einsum("thd,shd->hts", queries, keys_act, preferred_element_type=F32) * weight
    inner_part = jnp.einsum(
        "hts,shd->thd", scores.astype(BF), values_act, preferred_element_type=F32
    )
    entry_decay = jnp.exp(-rate_vec[None, :] * (local_pos[:, None] + 1.0))
    carried_part = entry_decay[:, :, None] * jnp.einsum(
        "thd,hde->the", queries, carried.astype(BF), preferred_element_type=F32
    )
    attended = inner_part + carried_part
    mean_square = jnp.mean(attended * attended, axis=-1, keepdims=True)
    normed = attended * lax.rsqrt(mean_square + 1e-06) * norm_gain[None]
    hidden = (normed * jax.nn.sigmoid(gate_part)).astype(BF).reshape(rows, heads * size)

    def slot(origin):
        return (origin % 2 * 2 + origin // 2) * heads * size

    hidden_all = jnp.zeros((rows, 4 * heads * size), BF)
    hidden_all = lax.dynamic_update_slice(hidden_all, hidden, (0, slot(y)))
    for step in (2, 1, 3):
        piece = send(hidden, along_y(step))
        hidden_all = lax.dynamic_update_slice(hidden_all, piece, (0, slot((y + 4 - step) % 4)))

    span = 2 * heads * size
    w_out_all = w_out_all.reshape(4, span, -1)
    near, far = hidden_all[:, :span], hidden_all[:, span:]

    def columns_first(weights, rows_first):
        return lax.dot_general(
            weights, rows_first, (((0,), (1,)), ((), ())), preferred_element_type=F32
        )

    blocks = jnp.stack(
        [columns_first(w_out_all[p], near) + columns_first(w_out_all[2 + p], far) for p in range(2)]
    ).reshape(4, 2, -1, rows)
    kept = jnp.where(core == 0, blocks[:, 0], blocks[:, 1])
    given = jnp.where(core == 0, blocks[:, 1], blocks[:, 0]).astype(BF)
    summed = kept + send(given, other_core).astype(F32)
    total = lax.dynamic_index_in_dim(summed, zh, 0, False)
    outgoing = summed.astype(BF)
    for step in (2, 1, 3):
        piece = lax.dynamic_index_in_dim(outgoing, (zh + step) % 4, 0, False)
        total += send(piece, along_zh(step)).astype(F32)
    return total.astype(BF).T


def solution(mesh):
    fine = Mesh(mesh.devices.reshape(SIZES), AXES)
    row, col = ("zl", "x"), ("y", "zh", "core")
    in_specs = (P(row, col), P(row, col, None), P(col, None, row), P(col, None), P(col))
    return jax.shard_map(
        local, mesh=fine, in_specs=in_specs, out_specs=P(row, col), check_vma=False
    )
```

```python
import math

import jax
import jax.numpy as jnp
import numpy as np
from jax import lax
from jax.sharding import Mesh
from jax.sharding import PartitionSpec as P

NSLOPE = 16
AXES = ("zl", "x", "y", "zh", "core")
SIZES = (2, 4, 4, 4, 2)
BF = jnp.bfloat16
F32 = jnp.float32


def moves(target):
    pairs = []
    for flat in range(int(np.prod(SIZES))):
        place = [int(v) for v in np.unravel_index(flat, SIZES)]
        there = target(*place)
        if there is not None:
            pairs.append((flat, int(np.ravel_multi_index(there, SIZES))))
    return pairs


def send(array, target):
    return lax.ppermute(array, AXES, moves(target))


def along_x(step):
    return lambda zl, x, y, zh, c: (zl, (x + step) % 4, y, zh, c)


def along_y(step):
    return lambda zl, x, y, zh, c: (zl, x, (y + step) % 4, zh, c)


def along_zh(step):
    return lambda zl, x, y, zh, c: (zl, x, y, (zh + step) % 4, c)


def other_zl(zl, x, y, zh, c):
    return (1 - zl, x, y, zh, c)


def other_core(zl, x, y, zh, c):
    return (zl, x, y, zh, 1 - c)


def later_half(zl, x, y, zh, c):
    return (1, x, y, zh, c) if zl == 0 else None


def tokens_to_half(zl, x, y, zh, c):
    half = y // 2
    return (half, x, (zl ^ half) * 2 + y % 2, zh, c)


def w_out_to_columns(high):
    def target(zl, x, y, zh, c):
        return (zl, (y % 2) * 2 + x % 2, zl * 2 + x // 2, zh, c) if y // 2 == high else None

    return target


def w_out_to_other_zl(zl, x, y, zh, c):
    return (1 - zl, x, y, zh, c) if y // 2 == zl else None


def gather_ring(block, axis, along, half, other):
    left = send(block, along(1))
    right = send(block, along(-1))
    far_low = send(after(left[:half], other), along(1))
    far_high = send(right[half:], along(-1))
    place = lax.axis_index(axis)
    return (
        (block, 0, place),
        (left, 0, (place + 3) % 4),
        (right, 0, (place + 1) % 4),
        (far_low, 0, (place + 2) % 4),
        (far_high, half, (place + 2) % 4),
    )


def after(array, other):
    return array + other[(0,) * other.ndim] * jnp.zeros((), array.dtype)


def decay_rates(index_vec, total_rows):
    exponent = index_vec.astype(F32) / (NSLOPE - 1)
    fast_rate = 1.0 / 32.0
    slow_rate = 0.5 / total_rows
    return fast_rate * jnp.exp(exponent * math.log(slow_rate / fast_rate))


def local(tokens, w_qkvg, w_out, norm_gain, decay_index):
    rows = tokens.shape[0]
    heads = w_qkvg.shape[1]
    size = w_qkvg.shape[2] // 4
    core = lax.axis_index("core")
    zh = lax.axis_index("zh")
    y = lax.axis_index("y")

    w_out_block = w_out.reshape(heads * size, -1)
    w_out_moved = jnp.stack([send(w_out_block, w_out_to_columns(high)) for high in range(2)])

    moved = send(tokens.T, tokens_to_half)
    w_block = w_qkvg.reshape(2, 2, tokens.shape[1], -1)
    kv_cuts = [(4 * h + 1, 4 * h + 3) for h in range(heads)]
    qg_cuts = [(0, 1)] + [(4 * h + 3, 4 * h + 5) for h in range(heads - 1)] + [(4 * heads - 1, 4 * heads)]
    w_block = jnp.concatenate(
        [w_block[..., low * size : high * size] for low, high in kv_cuts + qg_cuts], axis=-1
    )
    w_block = jnp.stack(
        [jnp.where(core == own, w_block[:, 0], w_block[:, 1]) for own in range(2)], axis=1
    ).reshape(w_qkvg.shape[0], -1)
    weight_cols = lax.all_gather(after(w_block, moved), "x", axis=0, tiled=True)

    depth, across = moved.shape
    stacked = jnp.zeros((4, depth, across), BF)
    stacked = lax.dynamic_update_slice(stacked, moved[None], (zh, 0, 0))
    for step in (2, 1, 3):
        piece = send(moved, along_zh(step))
        stacked = lax.dynamic_update_slice(stacked, piece[None], ((zh + 4 - step) % 4, 0, 0))
    gathered = jnp.zeros((4, 4, 2, depth, across), BF)
    swapped = []
    for piece, start, place in gather_ring(stacked, "y", along_y, 2, w_out_moved):
        swapped.append(send(piece, other_core))
        both = jnp.stack([piece, swapped[-1]], axis=1)
        gathered = lax.dynamic_update_slice(gathered, both[None], (place, start, 0, 0, 0))
    gathered = gathered.reshape(2, 16 * depth, across)
    mine, theirs = gathered[0], gathered[1]

    w_out_pair = w_out_moved + send(w_out_moved, w_out_to_other_zl)
    w_out_all = lax.all_gather(w_out_pair, "x", axis=0, tiled=True)
    weight_cols = after(weight_cols, swapped[0])

    def projection(a, b):
        return lax.dot_general(a, b, (((0,), (0,)), ((), ())), preferred_element_type=F32)

    w_kv, w_qg = jnp.split(weight_cols, 2, axis=1)
    kv_theirs = projection(theirs, w_kv).astype(BF)
    kv_sent = send(kv_theirs, other_zl)
    qg_sent = send(projection(theirs, w_qg).astype(BF), other_zl)
    kv_own, qg_own = jnp.split(projection(mine, weight_cols), 2, axis=1)
    kv = (kv_own + kv_sent.astype(F32)).astype(BF).astype(F32)
    qg = (qg_own + qg_sent.astype(F32)).astype(BF).astype(F32)

    kv = jax.nn.silu(kv).reshape(rows, heads, 2, size)
    keys_act, values_act = kv[:, :, 0], kv[:, :, 1].astype(BF)
    rate_vec = decay_rates(decay_index, rows * 8)
    local_pos = jnp.arange(rows, dtype=F32)
    state_weight = jnp.exp(-rate_vec[None, :] * (rows - 1.0 - local_pos)[:, None])
    local_state = jnp.einsum(
        "shd,she->hde",
        (keys_act * state_weight[:, :, None]).astype(BF),
        values_act,
        preferred_element_type=F32,
    ).astype(BF)
    keys_act = keys_act.astype(BF)
    place = lax.axis_index("x")

    def power(count):
        return jnp.exp(-rate_vec * (rows * 1.0) * count)[:, None, None]

    carried = jnp.zeros(local_state.shape, F32)
    total = power((3 - place).astype(F32)) * local_state.astype(F32)
    for step in (2, 1, 3):
        earlier = send(local_state, along_x(step)).astype(F32)
        carried += jnp.where(place >= step, power(step - 1.0), 0.0) * earlier
        total += power((3 - (place + 4 - step) % 4).astype(F32)) * earlier
    carried += power(place.astype(F32)) * send(total.astype(BF), later_half).astype(F32)

    qg = after(qg, local_state).reshape(rows, heads, 2, size)
    queries, gate_part = jax.nn.silu(qg[:, :, 0]).astype(BF), qg[:, :, 1]
    distance = local_pos[:, None] - local_pos[None, :]
    weight = jnp.where(
        distance[None] >= 0,
        jnp.exp(-rate_vec[:, None, None] * jnp.maximum(distance, 0.0)[None]),
        0.0,
    )
    scores = jnp.einsum("thd,shd->hts", queries, keys_act, preferred_element_type=F32) * weight
    inner_part = jnp.einsum(
        "hts,shd->thd", scores.astype(BF), values_act, preferred_element_type=F32
    )
    entry_decay = jnp.exp(-rate_vec[None, :] * (local_pos[:, None] + 1.0))
    carried_part = entry_decay[:, :, None] * jnp.einsum(
        "thd,hde->the", queries, carried.astype(BF), preferred_element_type=F32
    )
    attended = inner_part + carried_part
    mean_square = jnp.mean(attended * attended, axis=-1, keepdims=True)
    normed = attended * lax.rsqrt(mean_square + 1e-06) * norm_gain[None]
    hidden = (normed * jax.nn.sigmoid(gate_part)).astype(BF).reshape(rows, heads * size)

    def slot(origin):
        return (origin % 2 * 2 + origin // 2) * heads * size

    hidden_all = jnp.zeros((rows, 4 * heads * size), BF)
    hidden_all = lax.dynamic_update_slice(hidden_all, hidden, (0, slot(y)))
    for step in (2, 1, 3):
        piece = send(hidden, along_y(step))
        hidden_all = lax.dynamic_update_slice(hidden_all, piece, (0, slot((y + 4 - step) % 4)))

    span = 2 * heads * size
    w_out_all = w_out_all.reshape(4, span, -1)
    near, far = hidden_all[:, :span], hidden_all[:, span:]

    def columns_first(weights, rows_first):
        return lax.dot_general(
            weights, rows_first, (((0,), (1,)), ((), ())), preferred_element_type=F32
        )

    blocks = jnp.stack(
        [columns_first(w_out_all[p], near) + columns_first(w_out_all[2 + p], far) for p in range(2)]
    ).reshape(4, 2, -1, rows)
    kept = jnp.where(core == 0, blocks[:, 0], blocks[:, 1])
    given = jnp.where(core == 0, blocks[:, 1], blocks[:, 0]).astype(BF)
    summed = kept + send(given, other_core).astype(F32)
    total = lax.dynamic_index_in_dim(summed, zh, 0, False)
    outgoing = summed.astype(BF)
    for step in (2, 1, 3):
        piece = lax.dynamic_index_in_dim(outgoing, (zh + step) % 4, 0, False)
        total += send(piece, along_zh(step)).astype(F32)
    return total.astype(BF).T


def solution(mesh):
    fine = Mesh(mesh.devices.reshape(SIZES), AXES)
    row, col = ("zl", "x"), ("y", "zh", "core")
    in_specs = (P(row, col), P(row, col, None), P(col, None, row), P(col, None), P(col))
    return jax.shard_map(
        local, mesh=fine, in_specs=in_specs, out_specs=P(row, col), check_vma=False
    )
```

```python
import math

import jax
import jax.numpy as jnp
import numpy as np
from jax import lax
from jax.sharding import Mesh
from jax.sharding import PartitionSpec as P

NSLOPE = 16
AXES = ("zl", "x", "y", "zh", "core")
SIZES = (2, 4, 4, 4, 2)
BF = jnp.bfloat16
F32 = jnp.float32


def moves(target):
    pairs = []
    for flat in range(int(np.prod(SIZES))):
        place = [int(v) for v in np.unravel_index(flat, SIZES)]
        there = target(*place)
        if there is not None:
            pairs.append((flat, int(np.ravel_multi_index(there, SIZES))))
    return pairs


def send(array, target):
    return lax.ppermute(array, AXES, moves(target))


def along_x(step):
    return lambda zl, x, y, zh, c: (zl, (x + step) % 4, y, zh, c)


def along_y(step):
    return lambda zl, x, y, zh, c: (zl, x, (y + step) % 4, zh, c)


def along_zh(step):
    return lambda zl, x, y, zh, c: (zl, x, y, (zh + step) % 4, c)


def other_zl(zl, x, y, zh, c):
    return (1 - zl, x, y, zh, c)


def other_core(zl, x, y, zh, c):
    return (zl, x, y, zh, 1 - c)


def later_half(zl, x, y, zh, c):
    return (1, x, y, zh, c) if zl == 0 else None


def tokens_to_half(zl, x, y, zh, c):
    half = y // 2
    return (half, x, (zl ^ half) * 2 + y % 2, zh, c)


def w_out_to_columns(high):
    def target(zl, x, y, zh, c):
        return (zl, (y % 2) * 2 + x % 2, zl * 2 + x // 2, zh, c) if y // 2 == high else None

    return target


def w_out_to_other_zl(zl, x, y, zh, c):
    return (1 - zl, x, y, zh, c) if y // 2 == zl else None


def gather_ring(block, axis, along, half, other):
    left = send(block, along(1))
    right = send(block, along(-1))
    far_low = send(after(left[:half], other), along(1))
    far_high = send(right[half:], along(-1))
    place = lax.axis_index(axis)
    return (
        (block, 0, place),
        (left, 0, (place + 3) % 4),
        (right, 0, (place + 1) % 4),
        (far_low, 0, (place + 2) % 4),
        (far_high, half, (place + 2) % 4),
    )


def after(array, other):
    return array + other[(0,) * other.ndim] * jnp.zeros((), array.dtype)


def decay_rates(index_vec, total_rows):
    exponent = index_vec.astype(F32) / (NSLOPE - 1)
    fast_rate = 1.0 / 32.0
    slow_rate = 0.5 / total_rows
    return fast_rate * jnp.exp(exponent * math.log(slow_rate / fast_rate))


def local(tokens, w_qkvg, w_out, norm_gain, decay_index):
    rows = tokens.shape[0]
    heads = w_qkvg.shape[1]
    size = w_qkvg.shape[2] // 4
    core = lax.axis_index("core")
    zh = lax.axis_index("zh")
    y = lax.axis_index("y")

    w_out_block = w_out.reshape(heads * size, -1)
    w_out_moved = jnp.stack([send(w_out_block, w_out_to_columns(high)) for high in range(2)])

    moved = send(tokens.T, tokens_to_half)
    w_block = w_qkvg.reshape(2, 2, tokens.shape[1], -1)
    kv_cuts = [(4 * h + 1, 4 * h + 3) for h in range(heads)]
    qg_cuts = [(4 * h, 4 * h + 1) for h in range(heads)] + [(4 * h + 3, 4 * h + 4) for h in range(heads)]
    w_block = jnp.concatenate(
        [w_block[..., low * size : high * size] for low, high in kv_cuts + qg_cuts], axis=-1
    )
    w_block = jnp.stack(
        [jnp.where(core == own, w_block[:, 0], w_block[:, 1]) for own in range(2)], axis=1
    ).reshape(w_qkvg.shape[0], -1)
    weight_cols = lax.all_gather(after(w_block, moved), "x", axis=0, tiled=True)

    depth, across = moved.shape
    stacked = jnp.zeros((4, depth, across), BF)
    stacked = lax.dynamic_update_slice(stacked, moved[None], (zh, 0, 0))
    for step in (2, 1, 3):
        piece = send(moved, along_zh(step))
        stacked = lax.dynamic_update_slice(stacked, piece[None], ((zh + 4 - step) % 4, 0, 0))
    gathered = jnp.zeros((4, 4, 2, depth, across), BF)
    swapped = []
    for piece, start, place in gather_ring(stacked, "y", along_y, 2, w_out_moved):
        swapped.append(send(piece, other_core))
        both = jnp.stack([piece, swapped[-1]], axis=1)
        gathered = lax.dynamic_update_slice(gathered, both[None], (place, start, 0, 0, 0))
    gathered = gathered.reshape(2, 16 * depth, across)
    mine, theirs = gathered[0], gathered[1]

    w_out_pair = w_out_moved + send(w_out_moved, w_out_to_other_zl)
    w_out_all = lax.all_gather(w_out_pair, "x", axis=0, tiled=True)
    weight_cols = after(weight_cols, swapped[0])

    def columns_first(weights, rows_last):
        return lax.dot_general(
            weights, rows_last, (((0,), (0,)), ((), ())), preferred_element_type=F32
        )

    w_kv, w_qg = jnp.split(weight_cols, 2, axis=1)
    kv_theirs = columns_first(w_kv, theirs).astype(BF)
    kv_sent = send(kv_theirs, other_zl)
    q_theirs, g_theirs = jnp.split(columns_first(w_qg, theirs).astype(BF), 2, axis=0)
    q_sent, g_sent = send(q_theirs, other_zl), send(g_theirs, other_zl)
    span = heads * size
    own_part = columns_first(weight_cols, mine)
    kv = (own_part[: 2 * span] + kv_sent.astype(F32)).astype(BF).astype(F32)
    q_part = (own_part[2 * span : 3 * span] + q_sent.astype(F32)).astype(BF).astype(F32)
    g_part = (own_part[3 * span :] + g_sent.astype(F32)).astype(BF).astype(F32)

    kv = jax.nn.silu(kv).reshape(heads, 2, size, rows)
    keys_act, values_act = kv[:, 0], kv[:, 1].astype(BF)
    rate_vec = decay_rates(decay_index, rows * 8)
    local_pos = jnp.arange(rows, dtype=F32)
    state_weight = jnp.exp(-rate_vec[:, None] * (rows - 1.0 - local_pos)[None, :])
    local_state = jnp.einsum(
        "hds,hes->hde",
        (keys_act * state_weight[:, None]).astype(BF),
        values_act,
        preferred_element_type=F32,
    ).astype(BF)
    keys_act = keys_act.astype(BF)
    place = lax.axis_index("x")

    def power(count):
        return jnp.exp(-rate_vec * (rows * 1.0) * count)[:, None, None]

    carried = jnp.zeros(local_state.shape, F32)
    total = power((3 - place).astype(F32)) * local_state.astype(F32)
    for step in (2, 1, 3):
        earlier = send(local_state, along_x(step)).astype(F32)
        carried += jnp.where(place >= step, power(step - 1.0), 0.0) * earlier
        total += power((3 - (place + 4 - step) % 4).astype(F32)) * earlier
    carried += power(place.astype(F32)) * send(total.astype(BF), later_half).astype(F32)

    queries = jax.nn.silu(after(q_part, local_state)).astype(BF).reshape(heads, size, rows)
    distance = local_pos[:, None] - local_pos[None, :]
    weight = jnp.where(
        distance[None] >= 0,
        jnp.exp(-rate_vec[:, None, None] * jnp.maximum(distance, 0.0)[None]),
        0.0,
    )
    scores = jnp.einsum("hdt,hds->hts", queries, keys_act, preferred_element_type=F32) * weight
    inner_part = jnp.einsum(
        "hts,hes->het", scores.astype(BF), values_act, preferred_element_type=F32
    )
    entry_decay = jnp.exp(-rate_vec[:, None] * (local_pos[None, :] + 1.0))
    carried_part = entry_decay[:, None] * jnp.einsum(
        "hdt,hde->het", queries, carried.astype(BF), preferred_element_type=F32
    )
    attended = inner_part + carried_part
    mean_square = jnp.mean(attended * attended, axis=1, keepdims=True)
    normed = attended * lax.rsqrt(mean_square + 1e-06) * norm_gain[:, :, None]
    gate = jax.nn.sigmoid(g_part.reshape(heads, size, rows))
    hidden = (normed * gate).astype(BF).reshape(span, rows)

    def slot(origin):
        return (origin % 2 * 2 + origin // 2) * heads * size

    hidden_all = jnp.zeros((4 * span, rows), BF)
    hidden_all = lax.dynamic_update_slice(hidden_all, hidden, (slot(y), 0))
    for step in (2, 1, 3):
        piece = send(hidden, along_y(step))
        if step == 2:
            w_out_all = after(w_out_all, piece)
        hidden_all = lax.dynamic_update_slice(hidden_all, piece, (slot((y + 4 - step) % 4), 0))

    w_out_all = w_out_all.reshape(4, 2 * span, -1)
    near, far = hidden_all[: 2 * span], hidden_all[2 * span :]

    blocks = jnp.stack(
        [columns_first(w_out_all[p], near) + columns_first(w_out_all[2 + p], far) for p in range(2)]
    ).reshape(4, 2, -1, rows)
    kept = jnp.where(core == 0, blocks[:, 0], blocks[:, 1])
    given = jnp.where(core == 0, blocks[:, 1], blocks[:, 0]).astype(BF)
    summed = kept + send(given, other_core).astype(F32)
    total = lax.dynamic_index_in_dim(summed, zh, 0, False)
    outgoing = summed.astype(BF)
    for step in (2, 1, 3):
        piece = lax.dynamic_index_in_dim(outgoing, (zh + step) % 4, 0, False)
        total += send(piece, along_zh(step)).astype(F32)
    return total.astype(BF).T


def solution(mesh):
    fine = Mesh(mesh.devices.reshape(SIZES), AXES)
    row, col = ("zl", "x"), ("y", "zh", "core")
    in_specs = (P(row, col), P(row, col, None), P(col, None, row), P(col, None), P(col))
    return jax.shard_map(
        local, mesh=fine, in_specs=in_specs, out_specs=P(row, col), check_vma=False
    )
```

```python
import math

import jax
import jax.numpy as jnp
import numpy as np
from jax import lax
from jax.sharding import Mesh
from jax.sharding import PartitionSpec as P

NSLOPE = 16
AXES = ("zl", "x", "y", "zh", "core")
SIZES = (2, 4, 4, 4, 2)
BF = jnp.bfloat16
F32 = jnp.float32


def moves(target):
    pairs = []
    for flat in range(int(np.prod(SIZES))):
        place = [int(v) for v in np.unravel_index(flat, SIZES)]
        there = target(*place)
        if there is not None:
            pairs.append((flat, int(np.ravel_multi_index(there, SIZES))))
    return pairs


def send(array, target):
    return lax.ppermute(array, AXES, moves(target))


def along_x(step):
    return lambda zl, x, y, zh, c: (zl, (x + step) % 4, y, zh, c)


def along_y(step):
    return lambda zl, x, y, zh, c: (zl, x, (y + step) % 4, zh, c)


def along_zh(step):
    return lambda zl, x, y, zh, c: (zl, x, y, (zh + step) % 4, c)


def other_zl(zl, x, y, zh, c):
    return (1 - zl, x, y, zh, c)


def other_core(zl, x, y, zh, c):
    return (zl, x, y, zh, 1 - c)


def later_half(zl, x, y, zh, c):
    return (1, x, y, zh, c) if zl == 0 else None


def tokens_to_half(zl, x, y, zh, c):
    half = y // 2
    return (half, x, (zl ^ half) * 2 + y % 2, zh, c)


def w_out_to_columns(high):
    def target(zl, x, y, zh, c):
        return (zl, (y % 2) * 2 + x % 2, zl * 2 + x // 2, zh, c) if y // 2 == high else None

    return target


def w_out_to_other_zl(zl, x, y, zh, c):
    return (1 - zl, x, y, zh, c) if y // 2 == zl else None


def gather_ring(block, axis, along, half, other):
    left = send(block, along(1))
    right = send(block, along(-1))
    far_low = send(after(left[:half], other), along(1))
    far_high = send(right[half:], along(-1))
    place = lax.axis_index(axis)
    return (
        (block, 0, place),
        (left, 0, (place + 3) % 4),
        (right, 0, (place + 1) % 4),
        (far_low, 0, (place + 2) % 4),
        (far_high, half, (place + 2) % 4),
    )


def after(array, other):
    return array + other[(0,) * other.ndim] * jnp.zeros((), array.dtype)


def decay_rates(index_vec, total_rows):
    exponent = index_vec.astype(F32) / (NSLOPE - 1)
    fast_rate = 1.0 / 32.0
    slow_rate = 0.5 / total_rows
    return fast_rate * jnp.exp(exponent * math.log(slow_rate / fast_rate))


def local(tokens, w_qkvg, w_out, norm_gain, decay_index):
    rows = tokens.shape[0]
    heads = w_qkvg.shape[1]
    size = w_qkvg.shape[2] // 4
    core = lax.axis_index("core")
    zh = lax.axis_index("zh")
    y = lax.axis_index("y")

    w_out_block = w_out.reshape(heads * size, -1)
    w_out_moved = jnp.stack([send(w_out_block, w_out_to_columns(high)) for high in range(2)])

    moved = send(tokens.T, tokens_to_half)
    w_block = w_qkvg.reshape(2, 2, tokens.shape[1], -1)
    kv_cuts = [(4 * h + 1, 4 * h + 3) for h in range(heads)]
    qg_cuts = [(4 * h, 4 * h + 1) for h in range(heads)] + [(4 * h + 3, 4 * h + 4) for h in range(heads)]
    w_block = jnp.concatenate(
        [w_block[..., low * size : high * size] for low, high in kv_cuts + qg_cuts], axis=-1
    )
    w_block = jnp.stack(
        [jnp.where(core == own, w_block[:, 0], w_block[:, 1]) for own in range(2)], axis=1
    ).reshape(w_qkvg.shape[0], -1)
    weight_cols = lax.all_gather(after(w_block, moved), "x", axis=0, tiled=True)

    depth, across = moved.shape
    stacked = jnp.zeros((4, depth, across), BF)
    stacked = lax.dynamic_update_slice(stacked, moved[None], (zh, 0, 0))
    for step in (1, 3, 2):
        piece = send(moved, along_zh(step))
        stacked = lax.dynamic_update_slice(stacked, piece[None], ((zh + 4 - step) % 4, 0, 0))
    gathered = jnp.zeros((4, 4, 2, depth, across), BF)
    swapped = []
    for piece, start, place in gather_ring(stacked, "y", along_y, 2, w_out_moved):
        swapped.append(send(piece, other_core))
        both = jnp.stack([piece, swapped[-1]], axis=1)
        gathered = lax.dynamic_update_slice(gathered, both[None], (place, start, 0, 0, 0))
    gathered = gathered.reshape(2, 16 * depth, across)
    mine, theirs = gathered[0], gathered[1]

    w_out_pair = w_out_moved + send(w_out_moved, w_out_to_other_zl)
    w_out_all = lax.all_gather(w_out_pair, "x", axis=0, tiled=True)
    weight_cols = after(weight_cols, swapped[0])

    def columns_first(weights, rows_last):
        return lax.dot_general(
            weights, rows_last, (((0,), (0,)), ((), ())), preferred_element_type=F32
        )

    w_kv, w_qg = jnp.split(weight_cols, 2, axis=1)
    kv_theirs = columns_first(w_kv, theirs).astype(BF)
    kv_sent = send(kv_theirs, other_zl)
    q_theirs, g_theirs = jnp.split(columns_first(w_qg, theirs).astype(BF), 2, axis=0)
    q_sent, g_sent = send(q_theirs, other_zl), send(g_theirs, other_zl)
    span = heads * size
    own_part = columns_first(weight_cols, mine)
    kv = (own_part[: 2 * span] + kv_sent.astype(F32)).astype(BF).astype(F32)
    q_part = (own_part[2 * span : 3 * span] + q_sent.astype(F32)).astype(BF).astype(F32)
    g_part = (own_part[3 * span :] + g_sent.astype(F32)).astype(BF).astype(F32)

    kv = jax.nn.silu(kv).reshape(heads, 2, size, rows)
    keys_act, values_act = kv[:, 0], kv[:, 1].astype(BF)
    rate_vec = decay_rates(decay_index, rows * 8)
    local_pos = jnp.arange(rows, dtype=F32)
    state_weight = jnp.exp(-rate_vec[:, None] * (rows - 1.0 - local_pos)[None, :])
    local_state = jnp.einsum(
        "hds,hes->hde",
        (keys_act * state_weight[:, None]).astype(BF),
        values_act,
        preferred_element_type=F32,
    ).astype(BF)
    keys_act = keys_act.astype(BF)
    place = lax.axis_index("x")

    def power(count):
        return jnp.exp(-rate_vec * (rows * 1.0) * count)[:, None, None]

    carried = jnp.zeros(local_state.shape, F32)
    total = power((3 - place).astype(F32)) * local_state.astype(F32)
    for step in (2, 1, 3):
        earlier = send(local_state, along_x(step)).astype(F32)
        carried += jnp.where(place >= step, power(step - 1.0), 0.0) * earlier
        total += power((3 - (place + 4 - step) % 4).astype(F32)) * earlier
    carried += power(place.astype(F32)) * send(total.astype(BF), later_half).astype(F32)

    queries = jax.nn.silu(after(q_part, local_state)).astype(BF).reshape(heads, size, rows)
    distance = local_pos[:, None] - local_pos[None, :]
    weight = jnp.where(
        distance[None] >= 0,
        jnp.exp(-rate_vec[:, None, None] * jnp.maximum(distance, 0.0)[None]),
        0.0,
    )
    scores = jnp.einsum("hdt,hds->hts", queries, keys_act, preferred_element_type=F32) * weight
    inner_part = jnp.einsum(
        "hts,hes->het", scores.astype(BF), values_act, preferred_element_type=F32
    )
    entry_decay = jnp.exp(-rate_vec[:, None] * (local_pos[None, :] + 1.0))
    carried_part = entry_decay[:, None] * jnp.einsum(
        "hdt,hde->het", queries, carried.astype(BF), preferred_element_type=F32
    )
    attended = inner_part + carried_part
    mean_square = jnp.mean(attended * attended, axis=1, keepdims=True)
    normed = attended * lax.rsqrt(mean_square + 1e-06) * norm_gain[:, :, None]
    gate = jax.nn.sigmoid(g_part.reshape(heads, size, rows))
    hidden = (normed * gate).astype(BF).reshape(span, rows)

    def slot(origin):
        return (origin % 2 * 2 + origin // 2) * heads * size

    hidden_all = jnp.zeros((4 * span, rows), BF)
    hidden_all = lax.dynamic_update_slice(hidden_all, hidden, (slot(y), 0))
    for step in (1, 3, 2):
        piece = send(hidden, along_y(step))
        if step == 1:
            w_out_all = after(w_out_all, piece)
        hidden_all = lax.dynamic_update_slice(hidden_all, piece, (slot((y + 4 - step) % 4), 0))

    w_out_all = w_out_all.reshape(4, 2 * span, -1)
    near, far = hidden_all[: 2 * span], hidden_all[2 * span :]

    blocks = jnp.stack(
        [columns_first(w_out_all[p], near) + columns_first(w_out_all[2 + p], far) for p in range(2)]
    ).reshape(4, 2, -1, rows)
    kept = jnp.where(core == 0, blocks[:, 0], blocks[:, 1])
    given = jnp.where(core == 0, blocks[:, 1], blocks[:, 0]).astype(BF)
    summed = kept + send(given, other_core).astype(F32)
    total = lax.dynamic_index_in_dim(summed, zh, 0, False)
    outgoing = summed.astype(BF)
    for step in (1, 3, 2):
        piece = lax.dynamic_index_in_dim(outgoing, (zh + step) % 4, 0, False)
        total += send(piece, along_zh(step)).astype(F32)
    return total.astype(BF).T


def solution(mesh):
    fine = Mesh(mesh.devices.reshape(SIZES), AXES)
    row, col = ("zl", "x"), ("y", "zh", "core")
    in_specs = (P(row, col), P(row, col, None), P(col, None, row), P(col, None), P(col))
    return jax.shard_map(
        local, mesh=fine, in_specs=in_specs, out_specs=P(row, col), check_vma=False
    )
```

```python
import math

import jax
import jax.numpy as jnp
import numpy as np
from jax import lax
from jax.sharding import Mesh
from jax.sharding import PartitionSpec as P

NSLOPE = 16
AXES = ("zl", "x", "y", "zh", "core")
SIZES = (2, 4, 4, 4, 2)
BF = jnp.bfloat16
F32 = jnp.float32


def moves(target):
    pairs = []
    for flat in range(int(np.prod(SIZES))):
        place = [int(v) for v in np.unravel_index(flat, SIZES)]
        there = target(*place)
        if there is not None:
            pairs.append((flat, int(np.ravel_multi_index(there, SIZES))))
    return pairs


def send(array, target):
    return lax.ppermute(array, AXES, moves(target))


def along_x(step):
    return lambda zl, x, y, zh, c: (zl, (x + step) % 4, y, zh, c)


def along_y(step):
    return lambda zl, x, y, zh, c: (zl, x, (y + step) % 4, zh, c)


def along_zh(step):
    return lambda zl, x, y, zh, c: (zl, x, y, (zh + step) % 4, c)


def other_zl(zl, x, y, zh, c):
    return (1 - zl, x, y, zh, c)


def other_core(zl, x, y, zh, c):
    return (zl, x, y, zh, 1 - c)


def later_half(zl, x, y, zh, c):
    return (1, x, y, zh, c) if zl == 0 else None


def tokens_to_half(zl, x, y, zh, c):
    half = y // 2
    return (half, x, (zl ^ half) * 2 + y % 2, zh, c)


def w_out_to_columns(high):
    def target(zl, x, y, zh, c):
        return (zl, (y % 2) * 2 + x % 2, zl * 2 + x // 2, zh, c) if y // 2 == high else None

    return target


def w_out_to_other_zl(zl, x, y, zh, c):
    return (1 - zl, x, y, zh, c) if y // 2 == zl else None


def gather_ring(block, axis, along, half, other):
    left = send(block, along(1))
    right = send(block, along(-1))
    far_low = send(after(left[:half], other), along(1))
    far_high = send(right[half:], along(-1))
    place = lax.axis_index(axis)
    return (
        (block, 0, place),
        (left, 0, (place + 3) % 4),
        (right, 0, (place + 1) % 4),
        (far_low, 0, (place + 2) % 4),
        (far_high, half, (place + 2) % 4),
    )


def after(array, other):
    return array + other[(0,) * other.ndim] * jnp.zeros((), array.dtype)


def decay_rates(index_vec, total_rows):
    exponent = index_vec.astype(F32) / (NSLOPE - 1)
    fast_rate = 1.0 / 32.0
    slow_rate = 0.5 / total_rows
    return fast_rate * jnp.exp(exponent * math.log(slow_rate / fast_rate))


def local(tokens, w_qkvg, w_out, norm_gain, decay_index):
    rows = tokens.shape[0]
    heads = w_qkvg.shape[1]
    size = w_qkvg.shape[2] // 4
    core = lax.axis_index("core")
    zh = lax.axis_index("zh")
    y = lax.axis_index("y")

    moved = send(tokens.T, tokens_to_half)
    w_block = w_qkvg.reshape(2, 2, tokens.shape[1], -1)
    kv_cuts = [(4 * h + 1, 4 * h + 3) for h in range(heads)]
    qg_cuts = [(4 * h, 4 * h + 1) for h in range(heads)] + [(4 * h + 3, 4 * h + 4) for h in range(heads)]
    w_block = jnp.concatenate(
        [w_block[..., low * size : high * size] for low, high in kv_cuts + qg_cuts], axis=-1
    )
    w_block = jnp.stack(
        [jnp.where(core == own, w_block[:, 0], w_block[:, 1]) for own in range(2)], axis=1
    ).reshape(w_qkvg.shape[0], -1)
    weight_cols = lax.all_gather(after(w_block, moved), "x", axis=0, tiled=True)

    depth, across = moved.shape
    stacked = jnp.zeros((4, depth, across), BF)
    stacked = lax.dynamic_update_slice(stacked, moved[None], (zh, 0, 0))
    for step in (1, 3, 2):
        piece = send(moved, along_zh(step))
        stacked = lax.dynamic_update_slice(stacked, piece[None], ((zh + 4 - step) % 4, 0, 0))
    w_out_block = w_out.reshape(heads * size, -1)
    w_out_moved = jnp.stack([send(w_out_block, w_out_to_columns(high)) for high in range(2)])

    gathered = jnp.zeros((4, 4, 2, depth, across), BF)
    swapped = []
    for piece, start, place in gather_ring(stacked, "y", along_y, 2, w_out_moved):
        swapped.append(send(piece, other_core))
        both = jnp.stack([piece, swapped[-1]], axis=1)
        gathered = lax.dynamic_update_slice(gathered, both[None], (place, start, 0, 0, 0))
    gathered = gathered.reshape(2, 16 * depth, across)
    mine, theirs = gathered[0], gathered[1]

    w_out_pair = w_out_moved + send(w_out_moved, w_out_to_other_zl)
    w_out_all = lax.all_gather(w_out_pair, "x", axis=0, tiled=True)
    weight_cols = after(weight_cols, swapped[0])

    def columns_first(weights, rows_last):
        return lax.dot_general(
            weights, rows_last, (((0,), (0,)), ((), ())), preferred_element_type=F32
        )

    w_kv, w_qg = jnp.split(weight_cols, 2, axis=1)
    kv_theirs = columns_first(w_kv, theirs).astype(BF)
    kv_sent = send(kv_theirs, other_zl)
    q_theirs, g_theirs = jnp.split(columns_first(w_qg, theirs).astype(BF), 2, axis=0)
    q_sent, g_sent = send(q_theirs, other_zl), send(g_theirs, other_zl)
    span = heads * size
    own_part = columns_first(weight_cols, mine)
    kv = (own_part[: 2 * span] + kv_sent.astype(F32)).astype(BF).astype(F32)
    q_part = (own_part[2 * span : 3 * span] + q_sent.astype(F32)).astype(BF).astype(F32)
    g_part = (own_part[3 * span :] + g_sent.astype(F32)).astype(BF).astype(F32)

    kv = jax.nn.silu(kv).reshape(heads, 2, size, rows)
    keys_act, values_act = kv[:, 0], kv[:, 1].astype(BF)
    rate_vec = decay_rates(decay_index, rows * 8)
    local_pos = jnp.arange(rows, dtype=F32)
    state_weight = jnp.exp(-rate_vec[:, None] * (rows - 1.0 - local_pos)[None, :])
    local_state = jnp.einsum(
        "hds,hes->hde",
        (keys_act * state_weight[:, None]).astype(BF),
        values_act,
        preferred_element_type=F32,
    ).astype(BF)
    keys_act = keys_act.astype(BF)
    place = lax.axis_index("x")

    def power(count):
        return jnp.exp(-rate_vec * (rows * 1.0) * count)[:, None, None]

    carried = jnp.zeros(local_state.shape, F32)
    total = power((3 - place).astype(F32)) * local_state.astype(F32)
    for step in (2, 1, 3):
        earlier = send(local_state, along_x(step)).astype(F32)
        carried += jnp.where(place >= step, power(step - 1.0), 0.0) * earlier
        total += power((3 - (place + 4 - step) % 4).astype(F32)) * earlier
    carried += power(place.astype(F32)) * send(total.astype(BF), later_half).astype(F32)

    queries = jax.nn.silu(after(q_part, local_state)).astype(BF).reshape(heads, size, rows)
    distance = local_pos[:, None] - local_pos[None, :]
    weight = jnp.where(
        distance[None] >= 0,
        jnp.exp(-rate_vec[:, None, None] * jnp.maximum(distance, 0.0)[None]),
        0.0,
    )
    scores = jnp.einsum("hdt,hds->hts", queries, keys_act, preferred_element_type=F32) * weight
    inner_part = jnp.einsum(
        "hts,hes->het", scores.astype(BF), values_act, preferred_element_type=F32
    )
    entry_decay = jnp.exp(-rate_vec[:, None] * (local_pos[None, :] + 1.0))
    carried_part = entry_decay[:, None] * jnp.einsum(
        "hdt,hde->het", queries, carried.astype(BF), preferred_element_type=F32
    )
    attended = inner_part + carried_part
    mean_square = jnp.mean(attended * attended, axis=1, keepdims=True)
    normed = attended * lax.rsqrt(mean_square + 1e-06) * norm_gain[:, :, None]
    gate = jax.nn.sigmoid(g_part.reshape(heads, size, rows))
    hidden = (normed * gate).astype(BF).reshape(span, rows)

    def slot(origin):
        return (origin % 2 * 2 + origin // 2) * heads * size

    hidden_all = jnp.zeros((4 * span, rows), BF)
    hidden_all = lax.dynamic_update_slice(hidden_all, hidden, (slot(y), 0))
    for step in (1, 3, 2):
        piece = send(hidden, along_y(step))
        if step == 1:
            w_out_all = after(w_out_all, piece)
        hidden_all = lax.dynamic_update_slice(hidden_all, piece, (slot((y + 4 - step) % 4), 0))

    w_out_all = w_out_all.reshape(4, 2 * span, -1)
    near, far = hidden_all[: 2 * span], hidden_all[2 * span :]

    blocks = jnp.stack(
        [columns_first(w_out_all[p], near) + columns_first(w_out_all[2 + p], far) for p in range(2)]
    ).reshape(4, 2, -1, rows)
    kept = jnp.where(core == 0, blocks[:, 0], blocks[:, 1])
    given = jnp.where(core == 0, blocks[:, 1], blocks[:, 0]).astype(BF)
    summed = kept + send(given, other_core).astype(F32)
    total = lax.dynamic_index_in_dim(summed, zh, 0, False)
    outgoing = summed.astype(BF)
    for step in (1, 3, 2):
        piece = lax.dynamic_index_in_dim(outgoing, (zh + step) % 4, 0, False)
        total += send(piece, along_zh(step)).astype(F32)
    return total.astype(BF).T


def solution(mesh):
    fine = Mesh(mesh.devices.reshape(SIZES), AXES)
    row, col = ("zl", "x"), ("y", "zh", "core")
    in_specs = (P(row, col), P(row, col, None), P(col, None, row), P(col, None), P(col))
    return jax.shard_map(
        local, mesh=fine, in_specs=in_specs, out_specs=P(row, col), check_vma=False
    )
```
